32 devices in a mesh: groups: 2 (over y), dp: 4 (over z), mp: 2 (over x), sub: 2 (over core).
Axes of the slice: x: 2, y: 2, z: 4, core: 2. Of those that a mesh axis runs over, the one named last changes fastest.
Arguments:
- tokens_in: bfloat16 [128, 4096], P(('groups', 'dp'), ('mp', 'sub')), parts along dimension 0, may hold values from -6 to 6
- grad_out: bfloat16 [128, 4096], P(('groups', 'dp'), ('mp', 'sub')), parts along dimension 0, may hold values from -12 to 12
- sample_grad: bfloat16 [128, 4096], P(('groups', 'dp'), ('mp', 'sub')), parts along dimension 0, may hold values from -4.5 to 4.5
- gate_tiles: bfloat16 [256, 16, 128, 128], P(('groups', 'dp'), ('mp', 'sub')), parts along dimension 0, may hold values from -0.125 to 0.125
- up_tiles: bfloat16 [256, 16, 128, 128], P(('groups', 'dp'), ('mp', 'sub')), parts along dimension 0, may hold values from -0.125 to 0.125
- down_tiles: bfloat16 [256, 16, 128, 128], P(('groups', 'dp'), ('mp', 'sub')), parts along dimension 0, may hold values from -0.0625 to 0.0625
- block_index: int32 [6, 128, 16], P('groups', 'dp', ('mp', 'sub')), parts along dimension 0, may hold values from 0 to 31, as said below
- owner_map: int32 [4, 128, 16], P('groups', 'dp', ('mp', 'sub')), parts along dimension 0, may hold values from 0 to 3, as said below
- slot_map: int32 [4, 128, 16], P('groups', 'dp', ('mp', 'sub')), parts along dimension 0, may hold values from 0 to 383, as said below
- moment_state: bfloat16 [8, 4, 384, 128, 128], P(('groups', 'dp'), ('mp', 'sub')), parts along dimension 0, may hold values from -0.59765625 to 0.59765625
- curvature_state: bfloat16 [8, 4, 384, 128, 128], P(('groups', 'dp'), ('mp', 'sub')), parts along dimension 0, may hold values from 0.0099487305 to 1
Outputs:
- new_moment: bfloat16 [8, 4, 384, 128, 128], P(('groups', 'dp'), ('mp', 'sub')), parts along dimension 0
- new_curvature: bfloat16 [8, 4, 384, 128, 128], P(('groups', 'dp'), ('mp', 'sub')), parts along dimension 0
- update: bfloat16 [8, 4, 384, 128, 128], P(('groups', 'dp'), ('mp', 'sub')), parts along dimension 0
The draws below stay inside these ranges and needn't reach their ends.
There are 2 independent parts, one for each index of `groups`. The reference program is written for one: setup_inputs(seed, part) draws one part's arguments, and reference() takes and returns one part's arrays. A program takes and returns all parts, laid end to end along the dimension named above; each array names one. Nothing has to cross between parts.
Inputs may be any that keep to these rules, and one draw needn't show every extreme that they name: `block_index`: for each matrix m and hidden block c, the entries k with k // 4 = g are 4 distinct width blocks in [g * 8, (g + 1) * 8). `owner_map`: the blocks of one device are those with c // 32 equal to its dp index and k // 4 equal to its band. Of one device's gate and up blocks together, at most 128 have the same owner, and in every draw some device has exactly 128 with one owner. `slot_map`: within one band, blocks with the same owner have distinct slots; an owner receives at most 384 blocks of a band, and in every band some owner receives exactly 384.
All inputs are finite; a program needn't handle non-finite values.
Results may differ from the reference program's by a relative error of at most 0.035.
Values may be sent and summed in bfloat16 or wider, within the bound.
A program may use at most 320 MiB of HBM per device.

```python
import math
import jax
import jax.numpy as jnp
from jax import lax

D = 4096
FF = 16384
BLOCK = 128
TOKENS = 64
BANDS = 4
FB = 128
KEEP = 16
RB_DEV = 8
KEEP_DEV = 4
FB_DEV = 32
TILES_DEV = 256
OWN_CAP = 384
SEND_CAP = 128
N_DP = 4


def draw_block_index(key, part):
    scores = jax.random.randint(key, (3, FB, BANDS, RB_DEV), 0, 1 << 20) * RB_DEV + jnp.arange(RB_DEV, dtype=jnp.int32)
    ordering = jnp.argsort(scores, axis=-1, stable=True).astype(jnp.int32)
    chosen = ordering[..., :KEEP_DEV] + (jnp.arange(BANDS, dtype=jnp.int32) * RB_DEV)[:, None]
    return chosen.reshape(3, FB, KEEP).astype(jnp.int32)


def owner_band(band_key):
    subkeys = jax.random.split(band_key, 5)
    source_perm = jax.random.permutation(subkeys[0], N_DP).astype(jnp.int32)
    owner_perm = jax.random.permutation(subkeys[1], N_DP).astype(jnp.int32)
    spread = jax.random.randint(subkeys[2], (N_DP // 2,), 0, TILES_DEV // 2 + 1).at[0].set(TILES_DEV // 2)
    owner_loads = jnp.stack([TILES_DEV + spread, TILES_DEV - spread], axis=1).reshape(N_DP).astype(jnp.int32)
    starts = (jnp.cumsum(owner_loads) - owner_loads).astype(jnp.int32)
    places = jnp.arange(N_DP * TILES_DEV, dtype=jnp.int32)
    rank_of = (jnp.sum((starts[None, :] <= places[:, None]).astype(jnp.int32), axis=1) - 1).astype(jnp.int32)
    within = places - starts[rank_of]
    owner_of = owner_perm[rank_of]
    source_of = source_perm[places // SEND_CAP % N_DP]
    occasion = places // (SEND_CAP * N_DP) * SEND_CAP + places % SEND_CAP
    tile_scores = jax.random.randint(subkeys[3], (N_DP, TILES_DEV), 0, 1 << 20) * TILES_DEV + jnp.arange(TILES_DEV, dtype=jnp.int32)
    tile_perm = jnp.argsort(tile_scores, axis=1, stable=True).astype(jnp.int32)
    slot_scores = jax.random.randint(subkeys[4], (N_DP, OWN_CAP), 0, 1 << 20) * OWN_CAP + jnp.arange(OWN_CAP, dtype=jnp.int32)
    slot_perm = jnp.argsort(slot_scores, axis=1, stable=True).astype(jnp.int32)
    tile_of = tile_perm[source_of, occasion]
    slot_of = slot_perm[rank_of, within]
    owner_table = jnp.zeros((N_DP, TILES_DEV), jnp.int32).at[source_of, tile_of].set(owner_of)
    slot_table = jnp.zeros((N_DP, TILES_DEV), jnp.int32).at[source_of, tile_of].set(slot_of)
    return (owner_table, slot_table)


def owner_layout(key):
    band_keys = jax.random.split(jax.random.fold_in(key, 11), BANDS)
    owner_table, slot_table = jax.vmap(owner_band)(band_keys)

    def arrange(table):
        shaped = table.reshape(BANDS, N_DP, 2, FB_DEV, KEEP_DEV)
        return jnp.transpose(shaped, (2, 1, 3, 0, 4)).reshape(2, FB, KEEP).astype(jnp.int32)
    return (arrange(owner_table), arrange(slot_table))


def draw_owner_map(key, part):
    return owner_layout(key)[0]


def draw_slot_map(key, part):
    return owner_layout(key)[1]


def steps_of(key, dims, shards, low, high):
    level, own = 1.0, jax.random.fold_in(key, 6)
    for axis_at, shards_of in shards:
        steps = jnp.exp(jax.random.uniform(jax.random.fold_in(own, axis_at), (shards_of,), jnp.float32, low / len(shards), high / len(shards)))
        level = level * jnp.repeat(steps, dims[axis_at] // shards_of).reshape([-1 if axis == axis_at else 1 for axis in range(len(dims))])
    return level


def gaussian(key, dims, scale, limit, cuts=(), kind=jnp.bfloat16):
    result = scale * jax.random.normal(key, dims, jnp.float32)
    if cuts:
        result = result * steps_of(key, dims, cuts, -0.22, 0.18)
    return jnp.clip(result, -limit, limit).astype(kind)


def setup_inputs(seed: int = 0, part: int = 0) -> dict:
    seeds = jax.random.split(jax.random.key(seed), 12)
    part_keys = jax.random.split(jax.random.fold_in(seeds[11], part), 12)
    tokens_in = gaussian(part_keys[0], (TOKENS, D), 1.0, 6.0, ((0, 4), (1, 4)))
    grad_out = gaussian(part_keys[1], (TOKENS, D), 2.0, 12.0, ((0, 4), (1, 4)))
    sample_grad = gaussian(part_keys[2], (TOKENS, D), 0.75, 4.5, ((0, 4), (1, 4)))
    gate_tiles = gaussian(part_keys[3], (FB, KEEP, BLOCK, BLOCK), (D // 2) ** -0.5, 0.125, ((0, 4), (1, 4)))
    up_tiles = gaussian(part_keys[4], (FB, KEEP, BLOCK, BLOCK), (D // 2) ** -0.5, 0.125, ((0, 4), (1, 4)))
    down_tiles = gaussian(part_keys[5], (FB, KEEP, BLOCK, BLOCK), (FF // 2) ** -0.5, 0.0625, ((0, 4), (1, 4)))
    block_index = draw_block_index(jax.random.fold_in(jax.random.fold_in(seeds[11], part), 71), part)
    owner_map = draw_owner_map(jax.random.fold_in(jax.random.fold_in(seeds[11], part), 71), part)
    slot_map = draw_slot_map(jax.random.fold_in(jax.random.fold_in(seeds[11], part), 71), part)
    moment_state = gaussian(part_keys[9], (N_DP, BANDS, OWN_CAP, BLOCK, BLOCK), 0.1, 0.59765625, ((0, 4), (1, 4)))
    curvature_state = jnp.clip(jnp.exp(math.log(1.0) - 4.61031033 * jax.random.uniform(part_keys[10], (N_DP, BANDS, OWN_CAP, BLOCK, BLOCK), jnp.float32) ** steps_of(part_keys[10], (N_DP, BANDS, OWN_CAP, BLOCK, BLOCK), ((0, 4), (1, 4)), -0.2, 0.2)), 0.0099487305, 1.0).astype(jnp.bfloat16)
    return dict(tokens_in=tokens_in, grad_out=grad_out, sample_grad=sample_grad, gate_tiles=gate_tiles, up_tiles=up_tiles, down_tiles=down_tiles, block_index=block_index, owner_map=owner_map, slot_map=slot_map, moment_state=moment_state, curvature_state=curvature_state)


momentum_decay = 0.9
curvature_decay = 0.95
curvature_scale = 0.5


def select_blocks(matrix, row_list):
    shaped = matrix.reshape(matrix.shape[0], matrix.shape[1] // BLOCK, BLOCK)
    return jnp.take(shaped, row_list, axis=1)


def backward_signals(summed):
    gate_sum = summed[:, 0:FF]
    up_sum = summed[:, FF:2 * FF]
    hidden_grad = summed[:, 2 * FF:3 * FF]
    sample_hidden = summed[:, 3 * FF:4 * FF]
    sigmoid_gate = jax.nn.sigmoid(gate_sum)
    activation = gate_sum * sigmoid_gate
    gate_slope = up_sum * sigmoid_gate * (1.0 + gate_sum * (1.0 - sigmoid_gate))
    return jnp.concatenate([hidden_grad * gate_slope, hidden_grad * activation, sample_hidden * gate_slope, sample_hidden * activation], axis=1).astype(jnp.bfloat16)


def reference(tokens_in, grad_out, sample_grad, gate_tiles, up_tiles, down_tiles, block_index, owner_map, slot_map, moment_state, curvature_state):
    def one_band(accum, band):
        first = band * KEEP_DEV
        row_list = lax.dynamic_slice_in_dim(block_index, first, KEEP_DEV, 2)
        gate_band = lax.dynamic_slice_in_dim(gate_tiles, first, KEEP_DEV, 1).astype(jnp.float32)
        up_band = lax.dynamic_slice_in_dim(up_tiles, first, KEEP_DEV, 1).astype(jnp.float32)
        down_band = lax.dynamic_slice_in_dim(down_tiles, first, KEEP_DEV, 1).astype(jnp.float32)
        gate_rows = select_blocks(tokens_in, row_list[0]).astype(jnp.float32)
        up_rows = select_blocks(tokens_in, row_list[1]).astype(jnp.float32)
        grad_rows = select_blocks(grad_out, row_list[2]).astype(jnp.float32)
        sample_rows = select_blocks(sample_grad, row_list[2]).astype(jnp.float32)
        gate_part = jnp.einsum("tckd,ckde->tce", gate_rows, gate_band).reshape(TOKENS, FF)
        up_part = jnp.einsum("tckd,ckde->tce", up_rows, up_band).reshape(TOKENS, FF)
        down_part = jnp.einsum("tckd,cked->tce", grad_rows, down_band).reshape(TOKENS, FF)
        sample_part = jnp.einsum("tckd,cked->tce", sample_rows, down_band).reshape(TOKENS, FF)
        parts = jnp.concatenate([gate_part, up_part, down_part, sample_part], axis=1).astype(jnp.bfloat16)
        parts = lax.optimization_barrier(parts)
        return accum + parts.astype(jnp.float32), None

    start_sum = jnp.zeros((TOKENS, 4 * FF), jnp.float32)
    summed, _ = lax.scan(one_band, start_sum, jnp.arange(BANDS, dtype=jnp.int32))
    signals = backward_signals(summed).astype(jnp.float32)
    dgate = signals[:, 0:FF].reshape(TOKENS, FB, BLOCK)
    dup = signals[:, FF:2 * FF].reshape(TOKENS, FB, BLOCK)
    sgate = signals[:, 2 * FF:3 * FF].reshape(TOKENS, FB, BLOCK)
    supper = signals[:, 3 * FF:4 * FF].reshape(TOKENS, FB, BLOCK)

    def band_grads(band):
        first = band * KEEP_DEV
        row_list = lax.dynamic_slice_in_dim(block_index, first, KEEP_DEV, 2)
        gate_rows = select_blocks(tokens_in, row_list[0]).astype(jnp.float32)
        up_rows = select_blocks(tokens_in, row_list[1]).astype(jnp.float32)
        grad_gate = jnp.einsum("tckd,tce->ckde", gate_rows, dgate)
        hat_gate = jnp.einsum("tckd,tce->ckde", gate_rows, sgate)
        grad_up = jnp.einsum("tckd,tce->ckde", up_rows, dup)
        hat_up = jnp.einsum("tckd,tce->ckde", up_rows, supper)
        return jnp.stack([jnp.stack([grad_gate, hat_gate]), jnp.stack([grad_up, hat_up])]).astype(jnp.bfloat16)

    by_band = lax.map(band_grads, jnp.arange(BANDS, dtype=jnp.int32))
    tile_list = jnp.transpose(by_band, (1, 3, 0, 4, 2, 5, 6)).reshape(2, FB, KEEP, 2, BLOCK, BLOCK)
    band_of = (jnp.arange(KEEP, dtype=jnp.int32) // KEEP_DEV)[None, None, :]
    flat_index = ((owner_map * BANDS + band_of) * OWN_CAP + slot_map).astype(jnp.int32).reshape(-1)
    placed = jnp.zeros((N_DP * BANDS * OWN_CAP, 2, BLOCK, BLOCK), jnp.bfloat16)
    placed = placed.at[flat_index].set(tile_list.reshape(-1, 2, BLOCK, BLOCK))
    placed = placed.reshape(N_DP, BANDS, OWN_CAP, 2, BLOCK, BLOCK)
    grad_state = placed[:, :, :, 0].astype(jnp.float32)
    hat_state = placed[:, :, :, 1].astype(jnp.float32)
    moment = momentum_decay * moment_state.astype(jnp.float32) + (1.0 - momentum_decay) * grad_state
    curvature = curvature_decay * curvature_state.astype(jnp.float32) + (1.0 - curvature_decay) * hat_state * hat_state
    update = jnp.clip(moment / (curvature_scale * curvature), -1.0, 1.0)
    return (moment.astype(jnp.bfloat16), curvature.astype(jnp.bfloat16), update.astype(jnp.bfloat16))
```

```python
import functools

import jax
import jax.numpy as jnp
from jax import lax
from jax.experimental import pallas as pl
from jax.experimental.pallas import tpu as pltpu
from jax.sharding import PartitionSpec as P

MESH = pl.DeviceIdType.MESH
VMEM_BYTES = 60 * 1024 * 1024
ZERO_ROW = 15


def nt_dot(a, b):
    return lax.dot_general(a, b, (((1,), (1,)), ((), ())), preferred_element_type=jnp.float32)


def signals_kernel(
    n, chunks, index_ref, tokens_ref, grads_ref, samples_ref, gate_hbm, up_hbm, down_hbm, meta_ref,
    sig_ref, rows_ref, meta_all,
    acts, gate_v, up_v, down_v, parts, from_sib, pair, from_x,
    tile_sem, act_send, act_recv, meta_send, meta_recv, sib1_send, sib1_recv, pair_send, pair_recv,
    z_send, z_recv, x_send, x_recv, s_send, s_recv,
):
    z, x, s = lax.axis_index("dp"), lax.axis_index("mp"), lax.axis_index("sub")
    columns, keep = gate_v.shape[0], gate_v.shape[1]
    quarter = columns // 4
    per = quarter // chunks
    local_rows, block = tokens_ref.shape[0], gate_v.shape[-1]
    tokens = n * local_rows
    blocks = tokens_ref.shape[1] // block
    order = [2 * (1 - x) + (1 - s), 2 * (1 - x) + s, 2 * x + (1 - s), 2 * x + s]

    def load(t, m):
        where = pl.ds(order[t] * quarter, quarter)
        source, target = ((gate_hbm, gate_v), (up_hbm, up_v), (down_hbm, down_v))[m]
        return pltpu.make_async_copy(source.at[where], target.at[where], tile_sem.at[t, m])

    for t in range(4):
        for m in range(3):
            load(t, m).start()

    barrier = pltpu.get_barrier_semaphore()
    for d in range(1, n):
        pl.semaphore_signal(
            barrier, inc=1, device_id={"dp": lax.rem(z + d, n)}, device_id_type=MESH
        )
    pl.semaphore_signal(barrier, inc=1, device_id={"mp": 1 - x}, device_id_type=MESH)
    pl.semaphore_signal(barrier, inc=1, device_id={"sub": 1 - s}, device_id_type=MESH)

    own_rows = pl.ds(pl.multiple_of(z * local_rows, local_rows), local_rows)
    for a, ref in enumerate((tokens_ref, grads_ref, samples_ref)):
        for b in range(blocks):
            acts[a * blocks + b, own_rows, :] = ref[:, b * block : (b + 1) * block]
    meta_all[z] = meta_ref[...]
    pl.semaphore_wait(barrier, n + 1)

    def remote(source, target, send, recv, device):
        return pltpu.make_async_remote_copy(
            src_ref=source, dst_ref=target, send_sem=send, recv_sem=recv,
            device_id=device, device_id_type=MESH,
        )

    def act_copy(d, origin):
        where = pl.ds(pl.multiple_of(origin * local_rows, local_rows), local_rows)
        view = acts.at[:, where, :]
        return remote(
            view, view, act_send.at[d - 1], act_recv.at[d - 1], {"dp": lax.rem(z + d, n)}
        )

    def meta_copy(d, origin):
        view = meta_all.at[origin]
        return remote(
            view, view, meta_send.at[d - 1], meta_recv.at[d - 1], {"dp": lax.rem(z + d, n)}
        )

    for d in range(1, n):
        act_copy(d, z).start()
    for d in range(1, n):
        meta_copy(d, z).start()
    for d in range(1, n):
        act_copy(d, lax.rem(z + n - d, n)).wait_recv()

    def compute(c, at):
        def row(m, k):
            return lax.rem(index_ref[(m * columns + c) * keep + k], blocks)

        for m, tile_ref in ((0, gate_v), (1, up_v)):
            lhs = jnp.concatenate([acts[row(m, k)] for k in range(keep)], axis=1)
            rhs = tile_ref[c].reshape(keep * block, block)
            product = jnp.dot(lhs, rhs, preferred_element_type=jnp.float32)
            parts[at, m] = product.astype(jnp.bfloat16)
        total = None
        for k in range(keep):
            r = row(2, k)
            lhs = jnp.concatenate([acts[blocks + r], acts[2 * blocks + r]], axis=0)
            term = nt_dot(lhs, down_v[c, k])
            total = term if total is None else total + term
        parts[at, 2] = total[:tokens].astype(jnp.bfloat16)
        parts[at, 3] = total[tokens:].astype(jnp.bfloat16)

    def sib_part(i, j):
        return remote(
            parts.at[pl.ds(2 * i * quarter + j * per, per)],
            from_sib.at[pl.ds(i * quarter + j * per, per)],
            sib1_send.at[i, j], sib1_recv.at[i, j], {"sub": 1 - s},
        )

    def pair_copy(j):
        where = pl.ds(j * per, per)
        return remote(
            pair.at[where], from_x.at[where], pair_send.at[j], pair_recv.at[j], {"mp": 1 - x}
        )

    for t in range(4):
        for m in range(3):
            load(t, m).wait()

        def chunk_step(j, carry, t=t):
            def one(u, inner):
                cc = j * per + u
                compute(order[t] * quarter + cc, t * quarter + cc)
                return inner

            lax.fori_loop(0, per, one, 0)
            if t in (0, 2):
                sib_part(t // 2, j).start()
            if t == 1:
                sib_part(0, j).wait_recv()

                def add(u, inner):
                    cc = j * per + u
                    pair[cc] = (
                        parts[quarter + cc].astype(jnp.float32)
                        + from_sib[cc].astype(jnp.float32)
                    ).astype(jnp.bfloat16)
                    return inner

                lax.fori_loop(0, per, add, 0)
                pair_copy(j).start()
            return carry

        lax.fori_loop(0, chunks, chunk_step, 0)

    for b in range(blocks):
        rows_ref[b] = acts[b].astype(jnp.float32).T.astype(jnp.bfloat16)
    for b in range(blocks, rows_ref.shape[0]):
        rows_ref[b] = jnp.zeros(rows_ref.shape[1:], jnp.bfloat16)

    def place(origin, xq, sq, j):
        first = (origin * columns + (2 * xq + sq) * quarter + j * per) * 2
        return sig_ref.at[pl.ds(first, 2 * per)]

    def z_copy(way, d, j, origin):
        side = (1 - way) // 2
        view = place(origin, x, s, j)
        return remote(
            view, view, z_send.at[side, d - 1, j], z_recv.at[side, d - 1, j], {"dp": z + way}
        )

    def x_copy(xq, origin, j):
        view = place(origin, xq, s, j)
        return remote(view, view, x_send.at[origin, j], x_recv.at[origin, j], {"mp": 1 - x})

    def s_copy(xq, sq, origin, j):
        view = place(origin, xq, sq, j)
        return remote(
            view, view, s_send.at[xq, origin, j], s_recv.at[xq, origin, j], {"sub": 1 - s}
        )

    def inside(at):
        return (at >= 0) & (at < n)

    def produce(j):
        sib_part(1, j).wait_recv()
        pair_copy(j).wait_recv()

        def one(u, inner):
            cc = j * per + u
            gate_sum, up_sum, hidden, sample = [
                parts[3 * quarter + cc, a].astype(jnp.float32)
                + from_sib[quarter + cc, a].astype(jnp.float32)
                + from_x[cc, a].astype(jnp.float32)
                for a in range(4)
            ]
            sig = jax.nn.sigmoid(gate_sum)
            act = gate_sum * sig
            slope = up_sum * sig * (1.0 + gate_sum * (1.0 - sig))
            at = (z * columns + (2 * x + s) * quarter + cc) * 2
            sig_ref[at, :, 0:block] = (hidden * slope).astype(jnp.bfloat16)
            sig_ref[at, :, block : 2 * block] = (sample * slope).astype(jnp.bfloat16)
            sig_ref[at + 1, :, 0:block] = (hidden * act).astype(jnp.bfloat16)
            sig_ref[at + 1, :, block : 2 * block] = (sample * act).astype(jnp.bfloat16)
            return inner

        lax.fori_loop(0, per, one, 0)

    def x_arrivals(d, j):
        for way in (1, -1) if d else (1,):
            origin = z - way * d

            @pl.when(inside(origin))
            def _():
                x_copy(1 - x, origin, j).wait_recv()
                s_copy(1 - x, s, origin, j).start()

    for d in range(n):

        def spread(j, carry, d=d):
            if d == 0:
                produce(j)
                x_copy(x, z, j).start()
                for way in (1, -1):

                    @pl.when(inside(z + way))
                    def _():
                        z_copy(way, 1, j, z).start()

                s_copy(x, s, z, j).start()
                return carry
            for way in (1, -1):
                origin = z - way * d

                @pl.when(inside(origin))
                def _():
                    z_copy(way, d, j, origin).wait_recv()
                    if d < n - 1:

                        @pl.when(inside(z + way))
                        def _():
                            z_copy(way, d + 1, j, origin).start()

                    x_copy(x, origin, j).start()
                    s_copy(x, s, origin, j).start()

            x_arrivals(d - 1, j)
            return carry

        lax.fori_loop(0, chunks, spread, 0)

    def finish(j, carry):
        x_arrivals(n - 1, j)
        return carry

    lax.fori_loop(0, chunks, finish, 0)

    for d in range(1, n):
        meta_copy(d, lax.rem(z + n - d, n)).wait_recv()
        act_copy(d, z).wait_send()
        meta_copy(d, z).wait_send()

    def drain(j, carry):
        sib_part(0, j).wait_send()
        sib_part(1, j).wait_send()
        pair_copy(j).wait_send()
        for d in range(1, n):
            for way in (1, -1):
                origin = z - way * (d - 1)

                @pl.when(inside(origin) & inside(z + way))
                def _():
                    z_copy(way, d, j, origin).wait_send()

        for origin in range(n):
            x_copy(x, origin, j).wait_send()
            for xq in range(2):
                s_copy(xq, s, origin, j).wait_send()
                s_copy(xq, 1 - s, origin, j).wait_recv()
        return carry

    lax.fori_loop(0, chunks, drain, 0)


def update_kernel(per_step, table_ref, sig_ref, rows_ref, moment_ref, curvature_ref, m_out, c_out, u_out):
    step = pl.program_id(0)
    block = moment_ref.shape[-1]

    def one(u, carry):
        code = table_ref[step * per_step + u]
        lhs = rows_ref[code & 15]
        rhs = sig_ref[code >> 4]
        product = jnp.dot(lhs, rhs, preferred_element_type=jnp.float32)
        product = product.astype(jnp.bfloat16).astype(jnp.float32)
        grad, hat = product[:, :block], product[:, block:]
        moment = 0.9 * moment_ref[u].astype(jnp.float32) + (1.0 - 0.9) * grad
        curvature = 0.95 * curvature_ref[u].astype(jnp.float32) + (1.0 - 0.95) * hat * hat
        m_out[u] = moment.astype(jnp.bfloat16)
        c_out[u] = curvature.astype(jnp.bfloat16)
        u_out[u] = jnp.clip(moment / (0.5 * curvature), -1.0, 1.0).astype(jnp.bfloat16)
        return carry

    lax.fori_loop(0, per_step, one, 0, unroll=4)


def factor_exchange(
    tokens_in, grad_out, sample_grad, gate_tiles, up_tiles, down_tiles,
    block_index, owner_map, slot_map, moment_state, curvature_state,
):
    n = lax.axis_size("dp")
    columns, keep, block, _ = gate_tiles.shape
    local_rows, width = tokens_in.shape
    tokens, blocks = n * local_rows, width // block
    own_cap = moment_state.shape[2]
    quarter = columns // 4
    chunks = 4
    z = lax.axis_index("dp")
    band = lax.axis_index(("mp", "sub"))
    key = owner_map * own_cap + slot_map
    column = z * columns + jnp.arange(columns, dtype=jnp.int32)
    entry = column[None, :, None] * 2 + jnp.arange(2, dtype=jnp.int32)[:, None, None]
    code = entry * 16 + block_index[:2] - band * blocks
    lanes = 2 * columns * keep // 8
    meta = jnp.stack([key.reshape(8, lanes), code.reshape(8, lanes)])
    vmem, hbm, smem = (
        pl.BlockSpec(memory_space=pltpu.VMEM),
        pl.BlockSpec(memory_space=pl.ANY),
        pl.BlockSpec(memory_space=pltpu.SMEM),
    )
    bf16, dma = jnp.bfloat16, pltpu.SemaphoreType.DMA
    sig, rows, meta_all = pl.pallas_call(
        functools.partial(signals_kernel, n, chunks),
        out_shape=(
            jax.ShapeDtypeStruct((n * columns * 2, tokens, 2 * block), bf16),
            jax.ShapeDtypeStruct((16, block, tokens), bf16),
            jax.ShapeDtypeStruct((n, 2, 8, lanes), jnp.int32),
        ),
        in_specs=[smem, vmem, vmem, vmem, hbm, hbm, hbm, vmem],
        out_specs=(vmem, vmem, vmem),
        scratch_shapes=[
            pltpu.VMEM((3 * blocks, tokens, block), bf16),
            pltpu.VMEM(gate_tiles.shape, bf16),
            pltpu.VMEM(gate_tiles.shape, bf16),
            pltpu.VMEM(gate_tiles.shape, bf16),
            pltpu.VMEM((columns, 4, tokens, block), bf16),
            pltpu.VMEM((2 * quarter, 4, tokens, block), bf16),
            pltpu.VMEM((quarter, 4, tokens, block), bf16),
            pltpu.VMEM((quarter, 4, tokens, block), bf16),
            dma((4, 3)),
            dma((n - 1,)), dma((n - 1,)), dma((n - 1,)), dma((n - 1,)),
            dma((2, chunks)), dma((2, chunks)), dma((chunks,)), dma((chunks,)),
            dma((2, n - 1, chunks)), dma((2, n - 1, chunks)),
            dma((n, chunks)), dma((n, chunks)),
            dma((2, n, chunks)), dma((2, n, chunks)),
        ],
        compiler_params=pltpu.CompilerParams(
            collective_id=0, has_side_effects=True, vmem_limit_bytes=VMEM_BYTES
        ),
        name="signals",
    )(
        block_index.reshape(-1), tokens_in, grad_out, sample_grad,
        gate_tiles, up_tiles, down_tiles, meta,
    )
    keys = meta_all[:, 0].reshape(-1) - z * own_cap
    codes = meta_all[:, 1].reshape(-1)
    match = keys[None, :] == jnp.arange(own_cap, dtype=jnp.int32)[:, None]
    table = jnp.sum(jnp.where(match, codes[None, :] - ZERO_ROW, 0), axis=1) + ZERO_ROW
    per_step = 16
    state = pl.BlockSpec((per_step, block, block), lambda i, t: (i, 0, 0))
    once = pl.Buffered(1)
    outs = pl.pallas_call(
        functools.partial(update_kernel, per_step),
        out_shape=[jax.ShapeDtypeStruct((own_cap, block, block), bf16)] * 3,
        grid_spec=pltpu.PrefetchScalarGridSpec(
            num_scalar_prefetch=1,
            grid=(own_cap // per_step,),
            in_specs=[
                pl.BlockSpec(sig.shape, lambda i, t: (0, 0, 0), pipeline_mode=once),
                pl.BlockSpec(rows.shape, lambda i, t: (0, 0, 0), pipeline_mode=once),
                state,
                state,
            ],
            out_specs=[state] * 3,
        ),
        compiler_params=pltpu.CompilerParams(vmem_limit_bytes=VMEM_BYTES),
        name="update",
    )(
        table, sig, rows,
        moment_state.reshape(own_cap, block, block),
        curvature_state.reshape(own_cap, block, block),
    )
    return tuple(out.reshape(moment_state.shape) for out in outs)


momentum_decay = 0.9
curvature_decay = 0.95
curvature_scale = 0.5


def pick_blocks(matrix, row_list, block_size):
    shaped = matrix.reshape(matrix.shape[0], matrix.shape[1] // block_size, block_size)
    chosen = row_list[..., None] == jnp.arange(shaped.shape[1], dtype=row_list.dtype)
    return jnp.einsum("tbd,ckb->tckd", shaped, chosen.astype(matrix.dtype))


def backward_signals(summed):
    hidden_width = summed.shape[1] // 4
    gate_sum = summed[:, 0:hidden_width]
    up_sum = summed[:, hidden_width : 2 * hidden_width]
    hidden_grad = summed[:, 2 * hidden_width : 3 * hidden_width]
    sample_hidden = summed[:, 3 * hidden_width : 4 * hidden_width]
    sigmoid_gate = jax.nn.sigmoid(gate_sum)
    activation = gate_sum * sigmoid_gate
    gate_slope = up_sum * sigmoid_gate * (1.0 + gate_sum * (1.0 - sigmoid_gate))
    return jnp.concatenate(
        [
            hidden_grad * gate_slope,
            hidden_grad * activation,
            sample_hidden * gate_slope,
            sample_hidden * activation,
        ],
        axis=1,
    ).astype(jnp.bfloat16)


def tile_exchange(
    tokens_in,
    grad_out,
    sample_grad,
    gate_tiles,
    up_tiles,
    down_tiles,
    block_index,
    owner_map,
    slot_map,
    moment_state,
    curvature_state,
):
    block_size = gate_tiles.shape[-1]
    column_count = gate_tiles.shape[0]
    band_blocks = tokens_in.shape[1] // block_size
    hidden_width = column_count * block_size
    all_tokens, all_grads, all_samples = (
        lax.all_gather(tokens_in, "dp", axis=0, tiled=True),
        lax.all_gather(grad_out, "dp", axis=0, tiled=True),
        lax.all_gather(sample_grad, "dp", axis=0, tiled=True),
    )
    token_count = all_tokens.shape[0]
    local_rows = block_index - lax.axis_index(("mp", "sub")) * band_blocks
    token_rows = all_tokens
    gate_part = jnp.einsum(
        "tckd,ckde->tce",
        pick_blocks(token_rows, local_rows[0], block_size),
        gate_tiles,
        preferred_element_type=jnp.float32,
    )
    up_part = jnp.einsum(
        "tckd,ckde->tce",
        pick_blocks(token_rows, local_rows[1], block_size),
        up_tiles,
        preferred_element_type=jnp.float32,
    )
    down_part = jnp.einsum(
        "tckd,cked->tce",
        pick_blocks(all_grads, local_rows[2], block_size),
        down_tiles,
        preferred_element_type=jnp.float32,
    )
    sample_part = jnp.einsum(
        "tckd,cked->tce",
        pick_blocks(all_samples, local_rows[2], block_size),
        down_tiles,
        preferred_element_type=jnp.float32,
    )
    summed = lax.psum(
        jnp.concatenate([gate_part, up_part, down_part, sample_part], axis=1)
        .reshape(token_count, 4 * hidden_width)
        .astype(jnp.bfloat16),
        ("mp", "sub"),
    ).astype(jnp.float32)
    shard_rows = backward_signals(summed)
    row_count = shard_rows.shape[0]
    token_rows = all_tokens
    gate_rows = pick_blocks(token_rows, local_rows[0], block_size)
    up_rows = pick_blocks(token_rows, local_rows[1], block_size)
    signals = shard_rows.reshape(row_count, 4, column_count, block_size)
    grad_gate = jnp.einsum(
        "tckd,tce->ckde", gate_rows, signals[:, 0], preferred_element_type=jnp.float32
    )
    grad_up = jnp.einsum(
        "tckd,tce->ckde", up_rows, signals[:, 1], preferred_element_type=jnp.float32
    )
    hat_gate = jnp.einsum(
        "tckd,tce->ckde", gate_rows, signals[:, 2], preferred_element_type=jnp.float32
    )
    hat_up = jnp.einsum(
        "tckd,tce->ckde", up_rows, signals[:, 3], preferred_element_type=jnp.float32
    )
    totals = jnp.stack([jnp.stack([grad_gate, grad_up]), jnp.stack([hat_gate, hat_up])])
    tile_list = jnp.transpose(totals.astype(jnp.bfloat16), (1, 2, 3, 0, 4, 5)).reshape(
        -1, 2, block_size, block_size
    )
    tile_total = tile_list.shape[0]
    owner_count = lax.axis_size("dp")
    own_cap = moment_state.shape[2]
    send_cap = max(2, 2 * (tile_total // owner_count))
    owners = owner_map.reshape(-1)
    slot_list = slot_map.reshape(-1)
    same_owner = owners[:, None] == owners[None, :]
    earlier = jnp.arange(tile_total)[None, :] < jnp.arange(tile_total)[:, None]
    send_rank = jnp.sum((same_owner & earlier).astype(jnp.int32), axis=1)
    position = owners * send_cap + send_rank
    payload = (
        jnp.zeros((owner_count * send_cap, 2, block_size, block_size), jnp.bfloat16)
        .at[position]
        .set(tile_list)
    )
    slot_ids = jnp.full((owner_count * send_cap,), own_cap, jnp.int32).at[position].set(slot_list)
    received, received_ids = (
        lax.all_to_all(
            payload.reshape(owner_count, send_cap, 2, block_size, block_size),
            "dp",
            split_axis=0,
            concat_axis=0,
            tiled=True,
        ),
        lax.all_to_all(
            slot_ids.reshape(owner_count, send_cap), "dp", split_axis=0, concat_axis=0, tiled=True
        ),
    )
    placed = jnp.zeros((own_cap + 1, 2, block_size, block_size), jnp.bfloat16)
    placed = placed.at[received_ids.reshape(-1)].set(
        received.reshape(-1, 2, block_size, block_size)
    )[:own_cap]
    grad_state = placed[:, 0].astype(jnp.float32)
    hat_state = placed[:, 1].astype(jnp.float32)
    state_shape = moment_state.shape
    moment = (
        momentum_decay * moment_state.reshape(own_cap, block_size, block_size).astype(jnp.float32)
        + (1.0 - momentum_decay) * grad_state
    )
    curvature = (
        curvature_decay
        * curvature_state.reshape(own_cap, block_size, block_size).astype(jnp.float32)
        + (1.0 - curvature_decay) * hat_state * hat_state
    )
    update = jnp.clip(moment / (curvature_scale * curvature), -1.0, 1.0)
    return (
        moment.astype(jnp.bfloat16).reshape(state_shape),
        curvature.astype(jnp.bfloat16).reshape(state_shape),
        update.astype(jnp.bfloat16).reshape(state_shape),
    )


def solution(mesh):
    in_specs = (
        P(("groups", "dp"), ("mp", "sub")),
        P(("groups", "dp"), ("mp", "sub")),
        P(("groups", "dp"), ("mp", "sub")),
        P(("groups", "dp"), ("mp", "sub"), None, None),
        P(("groups", "dp"), ("mp", "sub"), None, None),
        P(("groups", "dp"), ("mp", "sub"), None, None),
        P("groups", "dp", ("mp", "sub")),
        P("groups", "dp", ("mp", "sub")),
        P("groups", "dp", ("mp", "sub")),
        P(("groups", "dp"), ("mp", "sub"), None, None, None),
        P(("groups", "dp"), ("mp", "sub"), None, None, None),
    )
    out_specs = (
        P(("groups", "dp"), ("mp", "sub"), None, None, None),
        P(("groups", "dp"), ("mp", "sub"), None, None, None),
        P(("groups", "dp"), ("mp", "sub"), None, None, None),
    )
    factors = mesh.shape["mp"] == 2 and mesh.shape["sub"] == 2

    def on_device(*args):
        columns, _, block_size, _ = args[3].shape
        tokens = args[0].shape[0] * mesh.shape["dp"]
        own_cap = args[9].shape[2]
        fits = tokens <= block_size and columns % 16 == 0 and own_cap % 16 == 0
        return (factor_exchange if factors and fits else tile_exchange)(*args)

    return jax.shard_map(
        on_device, mesh=mesh, in_specs=in_specs, out_specs=out_specs, check_vma=False
    )
```

```python
import functools

import jax
import jax.numpy as jnp
from jax import lax
from jax.experimental import pallas as pl
from jax.experimental.pallas import tpu as pltpu
from jax.sharding import PartitionSpec as P

MESH = pl.DeviceIdType.MESH
VMEM_BYTES = 60 * 1024 * 1024
ZERO_ROW = 15


def nt_dot(a, b):
    return lax.dot_general(a, b, (((1,), (1,)), ((), ())), preferred_element_type=jnp.float32)


def signals_kernel(
    n, chunks, own_cap, index_ref, tokens_ref, grads_ref, samples_ref, gate_hbm, up_hbm, down_hbm,
    owner_ref, slot_ref, block_ref,
    sig_ref, rows_ref, table_ref,
    acts, meta_all, gate_v, up_v, down_v, parts, from_sib, pair, from_x,
    tile_sem, act_send, act_recv, meta_send, meta_recv, sib1_send, sib1_recv, pair_send, pair_recv,
    z_send, z_recv, x_send, x_recv, s_send, s_recv,
):
    z, x, s = lax.axis_index("dp"), lax.axis_index("mp"), lax.axis_index("sub")
    columns, keep = gate_v.shape[0], gate_v.shape[1]
    quarter = columns // 4
    per = quarter // chunks
    local_rows, block = tokens_ref.shape[0], gate_v.shape[-1]
    tokens = n * local_rows
    blocks = tokens_ref.shape[1] // block
    order = [2 * (1 - x) + (1 - s), 2 * (1 - x) + s, 2 * x + (1 - s), 2 * x + s]

    def load(t, m):
        where = pl.ds(order[t] * quarter, quarter)
        source, target = ((gate_hbm, gate_v), (up_hbm, up_v), (down_hbm, down_v))[m]
        return pltpu.make_async_copy(source.at[where], target.at[where], tile_sem.at[t, m])

    for t in range(4):
        for m in range(3):
            load(t, m).start()

    meta_all[...] = jnp.full(meta_all.shape, -1, jnp.int32)
    barrier = pltpu.get_barrier_semaphore()
    for d in range(1, n):
        pl.semaphore_signal(
            barrier, inc=1, device_id={"dp": lax.rem(z + d, n)}, device_id_type=MESH
        )
    pl.semaphore_signal(barrier, inc=1, device_id={"mp": 1 - x}, device_id_type=MESH)
    pl.semaphore_signal(barrier, inc=1, device_id={"sub": 1 - s}, device_id_type=MESH)

    own_rows = pl.ds(pl.multiple_of(z * local_rows, local_rows), local_rows)
    for a, ref in enumerate((tokens_ref, grads_ref, samples_ref)):
        for b in range(blocks):
            acts[a * blocks + b, own_rows, :] = ref[:, b * block : (b + 1) * block]
    lists = 2 * keep
    for m in range(2):
        column = lax.broadcasted_iota(jnp.int32, (keep, columns), 1) + z * columns
        code = (column * 2 + m) * 16 + block_ref[m] - (2 * x + s) * blocks
        key = owner_ref[m] * own_cap + slot_ref[m]
        for k in range(keep):
            at = pl.ds(z * lists + m * keep + k, 1)
            meta_all[0, at, 0:columns] = key[k : k + 1]
            meta_all[1, at, 0:columns] = code[k : k + 1]
    pl.semaphore_wait(barrier, n + 1)

    def remote(source, target, send, recv, device):
        return pltpu.make_async_remote_copy(
            src_ref=source, dst_ref=target, send_sem=send, recv_sem=recv,
            device_id=device, device_id_type=MESH,
        )

    def act_copy(d, origin):
        where = pl.ds(pl.multiple_of(origin * local_rows, local_rows), local_rows)
        view = acts.at[:, where, :]
        return remote(
            view, view, act_send.at[d - 1], act_recv.at[d - 1], {"dp": lax.rem(z + d, n)}
        )

    def meta_copy(d, origin):
        view = meta_all.at[:, pl.ds(pl.multiple_of(origin * lists, lists), lists), :]
        return remote(
            view, view, meta_send.at[d - 1], meta_recv.at[d - 1], {"dp": lax.rem(z + d, n)}
        )

    for d in range(1, n):
        act_copy(d, z).start()
    for d in range(1, n):
        meta_copy(d, z).start()
    for d in range(1, n):
        act_copy(d, lax.rem(z + n - d, n)).wait_recv()

    def compute(c, at):
        def row(m, k):
            return lax.rem(index_ref[m, k, c], blocks)

        for m, tile_ref in ((0, gate_v), (1, up_v)):
            lhs = jnp.concatenate([acts[row(m, k)] for k in range(keep)], axis=1)
            rhs = tile_ref[c].reshape(keep * block, block)
            product = jnp.dot(lhs, rhs, preferred_element_type=jnp.float32)
            parts[at, m] = product.astype(jnp.bfloat16)
        total = None
        for k in range(keep):
            r = row(2, k)
            lhs = jnp.concatenate([acts[blocks + r], acts[2 * blocks + r]], axis=0)
            term = nt_dot(lhs, down_v[c, k])
            total = term if total is None else total + term
        parts[at, 2] = total[:tokens].astype(jnp.bfloat16)
        parts[at, 3] = total[tokens:].astype(jnp.bfloat16)

    def sib_part(i, j):
        return remote(
            parts.at[pl.ds(2 * i * quarter + j * per, per)],
            from_sib.at[pl.ds(i * quarter + j * per, per)],
            sib1_send.at[i, j], sib1_recv.at[i, j], {"sub": 1 - s},
        )

    def pair_copy(j):
        where = pl.ds(j * per, per)
        return remote(
            pair.at[where], from_x.at[where], pair_send.at[j], pair_recv.at[j], {"mp": 1 - x}
        )

    for t in range(4):
        for m in range(3):
            load(t, m).wait()

        def chunk_step(j, carry, t=t):
            def one(u, inner):
                cc = j * per + u
                compute(order[t] * quarter + cc, t * quarter + cc)
                return inner

            lax.fori_loop(0, per, one, 0)
            if t in (0, 2):
                sib_part(t // 2, j).start()
            if t == 1:
                sib_part(0, j).wait_recv()

                def add(u, inner):
                    cc = j * per + u
                    pair[cc] = (
                        parts[quarter + cc].astype(jnp.float32)
                        + from_sib[cc].astype(jnp.float32)
                    ).astype(jnp.bfloat16)
                    return inner

                lax.fori_loop(0, per, add, 0)
                pair_copy(j).start()
            return carry

        lax.fori_loop(0, chunks, chunk_step, 0)

    for d in range(1, n):
        meta_copy(d, lax.rem(z + n - d, n)).wait_recv()
    keys = meta_all[0].astype(jnp.float32).T[:columns] - (z * own_cap).astype(jnp.float32)
    codes = meta_all[1].astype(jnp.float32).T[:columns] - ZERO_ROW
    slots = lax.broadcasted_iota(jnp.int32, (columns, own_cap), 1).astype(jnp.float32)
    found = jnp.zeros((columns, own_cap), jnp.float32)
    for r in range(n * lists):
        found += jnp.where(keys[:, r : r + 1] == slots, codes[:, r : r + 1], 0.0)
    table_ref[...] = (jnp.sum(found, axis=0, keepdims=True) + ZERO_ROW).astype(jnp.int32)

    for b in range(blocks):
        rows_ref[b] = acts[b].astype(jnp.float32).T.astype(jnp.bfloat16)
    for b in range(blocks, rows_ref.shape[0]):
        rows_ref[b] = jnp.zeros(rows_ref.shape[1:], jnp.bfloat16)

    shared = chunks // 4

    def place(origin, xq, sq, j):
        first = (origin * columns + (2 * xq + sq) * quarter + j * per) * 2
        return sig_ref.at[pl.ds(first, 2 * per)]

    def z_copy(way, d, j, origin, other=False):
        side = (1 - way) // 2
        view = place(origin, 1 - x if other else x, s, j)
        at = (side, d - 1, chunks + j if other else j)
        return remote(view, view, z_send.at[at], z_recv.at[at], {"dp": z + way})

    def x_copy(xq, origin, j):
        view = place(origin, xq, s, j)
        return remote(view, view, x_send.at[origin, j], x_recv.at[origin, j], {"mp": 1 - x})

    def s_copy(xq, sq, origin, j):
        view = place(origin, xq, sq, j)
        return remote(
            view, view, s_send.at[xq, origin, j], s_recv.at[xq, origin, j], {"sub": 1 - s}
        )

    def inside(at):
        return (at >= 0) & (at < n)

    def produce(j):
        sib_part(1, j).wait_recv()
        pair_copy(j).wait_recv()

        def one(u, inner):
            cc = j * per + u
            gate_sum, up_sum, hidden, sample = [
                parts[3 * quarter + cc, a].astype(jnp.float32)
                + from_sib[quarter + cc, a].astype(jnp.float32)
                + from_x[cc, a].astype(jnp.float32)
                for a in range(4)
            ]
            sig = jax.nn.sigmoid(gate_sum)
            act = gate_sum * sig
            slope = up_sum * sig * (1.0 + gate_sum * (1.0 - sig))
            at = (z * columns + (2 * x + s) * quarter + cc) * 2
            sig_ref[at, :, 0:block] = (hidden * slope).astype(jnp.bfloat16)
            sig_ref[at, :, block : 2 * block] = (sample * slope).astype(jnp.bfloat16)
            sig_ref[at + 1, :, 0:block] = (hidden * act).astype(jnp.bfloat16)
            sig_ref[at + 1, :, block : 2 * block] = (sample * act).astype(jnp.bfloat16)
            return inner

        lax.fori_loop(0, per, one, 0)

    def x_arrivals(d, j):
        for way in (1, -1) if d else (1,):
            origin = z - way * d

            @pl.when(inside(origin))
            def _():
                x_copy(1 - x, origin, j).wait_recv()
                s_copy(1 - x, s, origin, j).start()

    for d in range(n):

        def spread(j, carry, d=d):
            if d == 0:
                produce(j)
                x_copy(x, z, j).start()
                for way in (1, -1):

                    @pl.when(inside(z + way))
                    def _():
                        z_copy(way, 1, j, z).start()

                s_copy(x, s, z, j).start()
                return carry
            for way in (1, -1):
                origin = z - way * d

                @pl.when(inside(origin))
                def _():
                    z_copy(way, d, j, origin).wait_recv()
                    if d < n - 1:

                        @pl.when(inside(z + way))
                        def _():
                            z_copy(way, d + 1, j, origin).start()

                    @pl.when(j >= shared)
                    def _():
                        x_copy(x, origin, j).start()

                    s_copy(x, s, origin, j).start()

            @pl.when(j >= shared)
            def _():
                x_arrivals(d - 1, j)

            return carry

        lax.fori_loop(0, chunks, spread, 0)
        for f in range(shared):
            if d == 0:
                x_copy(1 - x, z, f).wait_recv()
            for way in (1, -1):
                origin = z - way * d

                @pl.when(inside(origin))
                def _():
                    if d > 0:
                        z_copy(way, d, f, origin, True).wait_recv()
                    if d < n - 1:

                        @pl.when(inside(z + way))
                        def _():
                            z_copy(way, d + 1, f, origin, True).start()

                    if d > 0:
                        s_copy(1 - x, s, origin, f).start()
            if d == 0:
                s_copy(1 - x, s, z, f).start()

    def finish(j, carry):
        x_arrivals(n - 1, j)
        return carry

    lax.fori_loop(shared, chunks, finish, 0)

    for d in range(1, n):
        act_copy(d, z).wait_send()
        meta_copy(d, z).wait_send()

    def drain(j, carry):
        sib_part(0, j).wait_send()
        sib_part(1, j).wait_send()
        pair_copy(j).wait_send()
        for d in range(1, n):
            for way in (1, -1):
                origin = z - way * (d - 1)

                @pl.when(inside(origin) & inside(z + way))
                def _():
                    z_copy(way, d, j, origin).wait_send()

                    @pl.when(j < shared)
                    def _():
                        z_copy(way, d, j, origin, True).wait_send()

        for origin in range(n):

            @pl.when((j >= shared) | (z == origin))
            def _():
                x_copy(x, origin, j).wait_send()

            for xq in range(2):
                s_copy(xq, s, origin, j).wait_send()
                s_copy(xq, 1 - s, origin, j).wait_recv()
        return carry

    lax.fori_loop(0, chunks, drain, 0)


def update_kernel(per_step, table_ref, sig_ref, rows_ref, moment_ref, curvature_ref, m_out, c_out, u_out):
    step = pl.program_id(0)
    block = moment_ref.shape[-1]

    def one(u, carry):
        code = table_ref[step * per_step + u]
        lhs = rows_ref[code & 15]
        rhs = sig_ref[code >> 4]
        product = jnp.dot(lhs, rhs, preferred_element_type=jnp.float32)
        product = product.astype(jnp.bfloat16).astype(jnp.float32)
        grad, hat = product[:, :block], product[:, block:]
        moment = 0.9 * moment_ref[u].astype(jnp.float32) + (1.0 - 0.9) * grad
        curvature = 0.95 * curvature_ref[u].astype(jnp.float32) + (1.0 - 0.95) * hat * hat
        m_out[u] = moment.astype(jnp.bfloat16)
        c_out[u] = curvature.astype(jnp.bfloat16)
        u_out[u] = jnp.clip(moment / (0.5 * curvature), -1.0, 1.0).astype(jnp.bfloat16)
        return carry

    lax.fori_loop(0, per_step, one, 0, unroll=16 if per_step % 16 == 0 else 1)


def factor_exchange(
    tokens_in, grad_out, sample_grad, gate_tiles, up_tiles, down_tiles,
    block_index, owner_map, slot_map, moment_state, curvature_state,
):
    n = lax.axis_size("dp")
    columns, keep, block, _ = gate_tiles.shape
    local_rows, width = tokens_in.shape
    tokens, blocks = n * local_rows, width // block
    own_cap = moment_state.shape[2]
    quarter = columns // 4
    chunks = 4
    owner_t, slot_t, index_t = [a.transpose(0, 2, 1) for a in (owner_map, slot_map, block_index)]
    vmem, hbm, smem = (
        pl.BlockSpec(memory_space=pltpu.VMEM),
        pl.BlockSpec(memory_space=pl.ANY),
        pl.BlockSpec(memory_space=pltpu.SMEM),
    )
    bf16, dma = jnp.bfloat16, pltpu.SemaphoreType.DMA
    sig, rows, table = pl.pallas_call(
        functools.partial(signals_kernel, n, chunks, own_cap),
        out_shape=(
            jax.ShapeDtypeStruct((n * columns * 2, tokens, 2 * block), bf16),
            jax.ShapeDtypeStruct((16, block, tokens), bf16),
            jax.ShapeDtypeStruct((1, own_cap), jnp.int32),
        ),
        in_specs=[smem, vmem, vmem, vmem, hbm, hbm, hbm, vmem, vmem, vmem],
        out_specs=(vmem, vmem, vmem),
        scratch_shapes=[
            pltpu.VMEM((3 * blocks, tokens, block), bf16),
            pltpu.VMEM((2, 128, 128), jnp.int32),
            pltpu.VMEM(gate_tiles.shape, bf16),
            pltpu.VMEM(gate_tiles.shape, bf16),
            pltpu.VMEM(gate_tiles.shape, bf16),
            pltpu.VMEM((columns, 4, tokens, block), bf16),
            pltpu.VMEM((2 * quarter, 4, tokens, block), bf16),
            pltpu.VMEM((quarter, 4, tokens, block), bf16),
            pltpu.VMEM((quarter, 4, tokens, block), bf16),
            dma((4, 3)),
            dma((n - 1,)), dma((n - 1,)), dma((n - 1,)), dma((n - 1,)),
            dma((2, chunks)), dma((2, chunks)), dma((chunks,)), dma((chunks,)),
            dma((2, n - 1, chunks + chunks // 4)), dma((2, n - 1, chunks + chunks // 4)),
            dma((n, chunks)), dma((n, chunks)),
            dma((2, n, chunks)), dma((2, n, chunks)),
        ],
        compiler_params=pltpu.CompilerParams(
            collective_id=0, has_side_effects=True, vmem_limit_bytes=VMEM_BYTES
        ),
        name="signals",
    )(
        index_t, tokens_in, grad_out, sample_grad,
        gate_tiles, up_tiles, down_tiles, owner_t, slot_t, index_t,
    )
    per_step = max(p for p in range(1, 65) if own_cap % p == 0)
    state = pl.BlockSpec((per_step, block, block), lambda i, t: (i, 0, 0))
    once = pl.Buffered(1)
    outs = pl.pallas_call(
        functools.partial(update_kernel, per_step),
        out_shape=[jax.ShapeDtypeStruct((own_cap, block, block), bf16)] * 3,
        grid_spec=pltpu.PrefetchScalarGridSpec(
            num_scalar_prefetch=1,
            grid=(own_cap // per_step,),
            in_specs=[
                pl.BlockSpec(sig.shape, lambda i, t: (0, 0, 0), pipeline_mode=once),
                pl.BlockSpec(rows.shape, lambda i, t: (0, 0, 0), pipeline_mode=once),
                state,
                state,
            ],
            out_specs=[state] * 3,
        ),
        compiler_params=pltpu.CompilerParams(vmem_limit_bytes=VMEM_BYTES),
        name="update",
    )(
        table.reshape(own_cap), sig, rows,
        moment_state.reshape(own_cap, block, block),
        curvature_state.reshape(own_cap, block, block),
    )
    return tuple(out.reshape(moment_state.shape) for out in outs)


momentum_decay = 0.9
curvature_decay = 0.95
curvature_scale = 0.5


def pick_blocks(matrix, row_list, block_size):
    shaped = matrix.reshape(matrix.shape[0], matrix.shape[1] // block_size, block_size)
    chosen = row_list[..., None] == jnp.arange(shaped.shape[1], dtype=row_list.dtype)
    return jnp.einsum("tbd,ckb->tckd", shaped, chosen.astype(matrix.dtype))


def backward_signals(summed):
    hidden_width = summed.shape[1] // 4
    gate_sum = summed[:, 0:hidden_width]
    up_sum = summed[:, hidden_width : 2 * hidden_width]
    hidden_grad = summed[:, 2 * hidden_width : 3 * hidden_width]
    sample_hidden = summed[:, 3 * hidden_width : 4 * hidden_width]
    sigmoid_gate = jax.nn.sigmoid(gate_sum)
    activation = gate_sum * sigmoid_gate
    gate_slope = up_sum * sigmoid_gate * (1.0 + gate_sum * (1.0 - sigmoid_gate))
    return jnp.concatenate(
        [
            hidden_grad * gate_slope,
            hidden_grad * activation,
            sample_hidden * gate_slope,
            sample_hidden * activation,
        ],
        axis=1,
    ).astype(jnp.bfloat16)


def tile_exchange(
    tokens_in,
    grad_out,
    sample_grad,
    gate_tiles,
    up_tiles,
    down_tiles,
    block_index,
    owner_map,
    slot_map,
    moment_state,
    curvature_state,
):
    block_size = gate_tiles.shape[-1]
    column_count = gate_tiles.shape[0]
    band_blocks = tokens_in.shape[1] // block_size
    hidden_width = column_count * block_size
    all_tokens, all_grads, all_samples = (
        lax.all_gather(tokens_in, "dp", axis=0, tiled=True),
        lax.all_gather(grad_out, "dp", axis=0, tiled=True),
        lax.all_gather(sample_grad, "dp", axis=0, tiled=True),
    )
    token_count = all_tokens.shape[0]
    local_rows = block_index - lax.axis_index(("mp", "sub")) * band_blocks
    token_rows = all_tokens
    gate_part = jnp.einsum(
        "tckd,ckde->tce",
        pick_blocks(token_rows, local_rows[0], block_size),
        gate_tiles,
        preferred_element_type=jnp.float32,
    )
    up_part = jnp.einsum(
        "tckd,ckde->tce",
        pick_blocks(token_rows, local_rows[1], block_size),
        up_tiles,
        preferred_element_type=jnp.float32,
    )
    down_part = jnp.einsum(
        "tckd,cked->tce",
        pick_blocks(all_grads, local_rows[2], block_size),
        down_tiles,
        preferred_element_type=jnp.float32,
    )
    sample_part = jnp.einsum(
        "tckd,cked->tce",
        pick_blocks(all_samples, local_rows[2], block_size),
        down_tiles,
        preferred_element_type=jnp.float32,
    )
    summed = lax.psum(
        jnp.concatenate([gate_part, up_part, down_part, sample_part], axis=1)
        .reshape(token_count, 4 * hidden_width)
        .astype(jnp.bfloat16),
        ("mp", "sub"),
    ).astype(jnp.float32)
    shard_rows = backward_signals(summed)
    row_count = shard_rows.shape[0]
    token_rows = all_tokens
    gate_rows = pick_blocks(token_rows, local_rows[0], block_size)
    up_rows = pick_blocks(token_rows, local_rows[1], block_size)
    signals = shard_rows.reshape(row_count, 4, column_count, block_size)
    grad_gate = jnp.einsum(
        "tckd,tce->ckde", gate_rows, signals[:, 0], preferred_element_type=jnp.float32
    )
    grad_up = jnp.einsum(
        "tckd,tce->ckde", up_rows, signals[:, 1], preferred_element_type=jnp.float32
    )
    hat_gate = jnp.einsum(
        "tckd,tce->ckde", gate_rows, signals[:, 2], preferred_element_type=jnp.float32
    )
    hat_up = jnp.einsum(
        "tckd,tce->ckde", up_rows, signals[:, 3], preferred_element_type=jnp.float32
    )
    totals = jnp.stack([jnp.stack([grad_gate, grad_up]), jnp.stack([hat_gate, hat_up])])
    tile_list = jnp.transpose(totals.astype(jnp.bfloat16), (1, 2, 3, 0, 4, 5)).reshape(
        -1, 2, block_size, block_size
    )
    tile_total = tile_list.shape[0]
    owner_count = lax.axis_size("dp")
    own_cap = moment_state.shape[2]
    send_cap = max(2, 2 * (tile_total // owner_count))
    owners = owner_map.reshape(-1)
    slot_list = slot_map.reshape(-1)
    same_owner = owners[:, None] == owners[None, :]
    earlier = jnp.arange(tile_total)[None, :] < jnp.arange(tile_total)[:, None]
    send_rank = jnp.sum((same_owner & earlier).astype(jnp.int32), axis=1)
    position = owners * send_cap + send_rank
    payload = (
        jnp.zeros((owner_count * send_cap, 2, block_size, block_size), jnp.bfloat16)
        .at[position]
        .set(tile_list)
    )
    slot_ids = jnp.full((owner_count * send_cap,), own_cap, jnp.int32).at[position].set(slot_list)
    received, received_ids = (
        lax.all_to_all(
            payload.reshape(owner_count, send_cap, 2, block_size, block_size),
            "dp",
            split_axis=0,
            concat_axis=0,
            tiled=True,
        ),
        lax.all_to_all(
            slot_ids.reshape(owner_count, send_cap), "dp", split_axis=0, concat_axis=0, tiled=True
        ),
    )
    placed = jnp.zeros((own_cap + 1, 2, block_size, block_size), jnp.bfloat16)
    placed = placed.at[received_ids.reshape(-1)].set(
        received.reshape(-1, 2, block_size, block_size)
    )[:own_cap]
    grad_state = placed[:, 0].astype(jnp.float32)
    hat_state = placed[:, 1].astype(jnp.float32)
    state_shape = moment_state.shape
    moment = (
        momentum_decay * moment_state.reshape(own_cap, block_size, block_size).astype(jnp.float32)
        + (1.0 - momentum_decay) * grad_state
    )
    curvature = (
        curvature_decay
        * curvature_state.reshape(own_cap, block_size, block_size).astype(jnp.float32)
        + (1.0 - curvature_decay) * hat_state * hat_state
    )
    update = jnp.clip(moment / (curvature_scale * curvature), -1.0, 1.0)
    return (
        moment.astype(jnp.bfloat16).reshape(state_shape),
        curvature.astype(jnp.bfloat16).reshape(state_shape),
        update.astype(jnp.bfloat16).reshape(state_shape),
    )


def solution(mesh):
    in_specs = (
        P(("groups", "dp"), ("mp", "sub")),
        P(("groups", "dp"), ("mp", "sub")),
        P(("groups", "dp"), ("mp", "sub")),
        P(("groups", "dp"), ("mp", "sub"), None, None),
        P(("groups", "dp"), ("mp", "sub"), None, None),
        P(("groups", "dp"), ("mp", "sub"), None, None),
        P("groups", "dp", ("mp", "sub")),
        P("groups", "dp", ("mp", "sub")),
        P("groups", "dp", ("mp", "sub")),
        P(("groups", "dp"), ("mp", "sub"), None, None, None),
        P(("groups", "dp"), ("mp", "sub"), None, None, None),
    )
    out_specs = (
        P(("groups", "dp"), ("mp", "sub"), None, None, None),
        P(("groups", "dp"), ("mp", "sub"), None, None, None),
        P(("groups", "dp"), ("mp", "sub"), None, None, None),
    )
    factors = mesh.shape["mp"] == 2 and mesh.shape["sub"] == 2

    def on_device(*args):
        columns, _, block_size, _ = args[3].shape
        tokens = args[0].shape[0] * mesh.shape["dp"]
        own_cap = args[9].shape[2]
        fits = tokens <= block_size and columns % 16 == 0 and own_cap % 16 == 0
        fits = fits and columns <= 128 and 2 * args[3].shape[1] * mesh.shape["dp"] <= 128
        return (factor_exchange if factors and fits else tile_exchange)(*args)

    return jax.shard_map(
        on_device, mesh=mesh, in_specs=in_specs, out_specs=out_specs, check_vma=False
    )
```

```python
import functools

import jax
import jax.numpy as jnp
from jax import lax
from jax.experimental import pallas as pl
from jax.experimental.pallas import tpu as pltpu
from jax.sharding import PartitionSpec as P

MESH = pl.DeviceIdType.MESH
VMEM_BYTES = 60 * 1024 * 1024
ZERO_ROW = 15


def nt_dot(a, b):
    return lax.dot_general(a, b, (((1,), (1,)), ((), ())), preferred_element_type=jnp.float32)


def signals_kernel(
    n, chunks, own_cap, index_ref, tokens_ref, grads_ref, samples_ref, gate_hbm, up_hbm, down_hbm,
    owner_ref, slot_ref, block_ref,
    sig_ref, rows_ref, table_ref,
    acts, meta_all, gate_v, up_v, down_v, parts, from_sib, pair, from_x,
    tile_sem, act_send, act_recv, meta_send, meta_recv, sib1_send, sib1_recv, pair_send, pair_recv,
    z_send, z_recv, x_send, x_recv, s_send, s_recv,
):
    z, x, s = lax.axis_index("dp"), lax.axis_index("mp"), lax.axis_index("sub")
    columns, keep = gate_v.shape[0], gate_v.shape[1]
    quarter = columns // 4
    per = quarter // chunks
    local_rows, block = tokens_ref.shape[0], gate_v.shape[-1]
    tokens = n * local_rows
    blocks = tokens_ref.shape[1] // block
    order = [2 * (1 - x) + (1 - s), 2 * (1 - x) + s, 2 * x + (1 - s), 2 * x + s]

    def load(t, m):
        where = pl.ds(order[t] * quarter, quarter)
        source, target = ((gate_hbm, gate_v), (up_hbm, up_v), (down_hbm, down_v))[m]
        return pltpu.make_async_copy(source.at[where], target.at[where], tile_sem.at[t, m])

    for t in range(4):
        for m in range(3):
            load(t, m).start()

    meta_all[...] = jnp.full(meta_all.shape, -1, jnp.int32)
    barrier = pltpu.get_barrier_semaphore()
    for d in range(1, n):
        pl.semaphore_signal(
            barrier, inc=1, device_id={"dp": lax.rem(z + d, n)}, device_id_type=MESH
        )
    pl.semaphore_signal(barrier, inc=1, device_id={"mp": 1 - x}, device_id_type=MESH)
    pl.semaphore_signal(barrier, inc=1, device_id={"sub": 1 - s}, device_id_type=MESH)

    own_rows = pl.ds(pl.multiple_of(z * local_rows, local_rows), local_rows)
    for a, ref in enumerate((tokens_ref, grads_ref, samples_ref)):
        for b in range(blocks):
            acts[a * blocks + b, own_rows, :] = ref[:, b * block : (b + 1) * block]
    lists = 2 * keep
    for m in range(2):
        column = lax.broadcasted_iota(jnp.int32, (keep, columns), 1) + z * columns
        code = (column * 2 + m) * 16 + block_ref[m] - (2 * x + s) * blocks
        key = owner_ref[m] * own_cap + slot_ref[m]
        for k in range(keep):
            at = pl.ds(z * lists + m * keep + k, 1)
            meta_all[0, at, 0:columns] = key[k : k + 1]
            meta_all[1, at, 0:columns] = code[k : k + 1]
    pl.semaphore_wait(barrier, n + 1)

    def remote(source, target, send, recv, device):
        return pltpu.make_async_remote_copy(
            src_ref=source, dst_ref=target, send_sem=send, recv_sem=recv,
            device_id=device, device_id_type=MESH,
        )

    def act_copy(d, origin):
        where = pl.ds(pl.multiple_of(origin * local_rows, local_rows), local_rows)
        view = acts.at[:, where, :]
        return remote(
            view, view, act_send.at[d - 1], act_recv.at[d - 1], {"dp": lax.rem(z + d, n)}
        )

    def meta_copy(d, origin):
        view = meta_all.at[:, pl.ds(pl.multiple_of(origin * lists, lists), lists), :]
        return remote(
            view, view, meta_send.at[d - 1], meta_recv.at[d - 1], {"dp": lax.rem(z + d, n)}
        )

    for d in range(1, n):
        act_copy(d, z).start()
    for d in range(1, n):
        meta_copy(d, z).start()
    for d in range(1, n):
        act_copy(d, lax.rem(z + n - d, n)).wait_recv()

    def compute(c, at):
        def row(m, k):
            return lax.rem(index_ref[m, k, c], blocks)

        for m, tile_ref in ((0, gate_v), (1, up_v)):
            lhs = jnp.concatenate([acts[row(m, k)] for k in range(keep)], axis=1)
            rhs = tile_ref[c].reshape(keep * block, block)
            product = jnp.dot(lhs, rhs, preferred_element_type=jnp.float32)
            parts[at, m] = product.astype(jnp.bfloat16)
        total = None
        for k in range(keep):
            r = row(2, k)
            lhs = jnp.concatenate([acts[blocks + r], acts[2 * blocks + r]], axis=0)
            term = nt_dot(lhs, down_v[c, k])
            total = term if total is None else total + term
        parts[at, 2] = total[:tokens].astype(jnp.bfloat16)
        parts[at, 3] = total[tokens:].astype(jnp.bfloat16)

    def sib_part(i, j):
        return remote(
            parts.at[pl.ds(2 * i * quarter + j * per, per)],
            from_sib.at[pl.ds(i * quarter + j * per, per)],
            sib1_send.at[i, j], sib1_recv.at[i, j], {"sub": 1 - s},
        )

    def pair_copy(j):
        where = pl.ds(j * per, per)
        return remote(
            pair.at[where], from_x.at[where], pair_send.at[j], pair_recv.at[j], {"mp": 1 - x}
        )

    for t in range(4):
        for m in range(3):
            load(t, m).wait()

        def chunk_step(j, carry, t=t):
            def one(u, inner):
                cc = j * per + u
                compute(order[t] * quarter + cc, t * quarter + cc)
                return inner

            lax.fori_loop(0, per, one, 0)
            if t in (0, 2):
                sib_part(t // 2, j).start()
            if t == 1:
                sib_part(0, j).wait_recv()

                def add(u, inner):
                    cc = j * per + u
                    pair[cc] = (
                        parts[quarter + cc].astype(jnp.float32)
                        + from_sib[cc].astype(jnp.float32)
                    ).astype(jnp.bfloat16)
                    return inner

                lax.fori_loop(0, per, add, 0)
                pair_copy(j).start()
            return carry

        lax.fori_loop(0, chunks, chunk_step, 0)

    for d in range(1, n):
        meta_copy(d, lax.rem(z + n - d, n)).wait_recv()
    keys = meta_all[0].astype(jnp.float32).T[:columns] - (z * own_cap).astype(jnp.float32)
    codes = meta_all[1].astype(jnp.float32).T[:columns] - ZERO_ROW
    slots = lax.broadcasted_iota(jnp.int32, (columns, own_cap), 1).astype(jnp.float32)
    found = jnp.zeros((columns, own_cap), jnp.float32)
    for r in range(n * lists):
        found += jnp.where(keys[:, r : r + 1] == slots, codes[:, r : r + 1], 0.0)
    table_ref[...] = (jnp.sum(found, axis=0, keepdims=True) + ZERO_ROW).astype(jnp.int32)

    for b in range(blocks):
        rows_ref[b] = acts[b].astype(jnp.float32).T.astype(jnp.bfloat16)
    for b in range(blocks, rows_ref.shape[0]):
        rows_ref[b] = jnp.zeros(rows_ref.shape[1:], jnp.bfloat16)

    shared = chunks // 4

    def place(origin, xq, sq, j):
        first = (origin * columns + (2 * xq + sq) * quarter + j * per) * 2
        return sig_ref.at[pl.ds(first, 2 * per)]

    def z_copy(way, d, j, origin, other=False):
        side = (1 - way) // 2
        view = place(origin, 1 - x if other else x, s, j)
        at = (side, d - 1, chunks + j if other else j)
        return remote(view, view, z_send.at[at], z_recv.at[at], {"dp": z + way})

    def x_copy(xq, origin, j):
        view = place(origin, xq, s, j)
        return remote(view, view, x_send.at[origin, j], x_recv.at[origin, j], {"mp": 1 - x})

    def s_copy(xq, sq, origin, j):
        view = place(origin, xq, sq, j)
        return remote(
            view, view, s_send.at[xq, origin, j], s_recv.at[xq, origin, j], {"sub": 1 - s}
        )

    def inside(at):
        return (at >= 0) & (at < n)

    def produce(j):
        sib_part(1, j).wait_recv()
        pair_copy(j).wait_recv()

        def one(u, inner):
            cc = j * per + u
            gate_sum, up_sum, hidden, sample = [
                parts[3 * quarter + cc, a].astype(jnp.float32)
                + from_sib[quarter + cc, a].astype(jnp.float32)
                + from_x[cc, a].astype(jnp.float32)
                for a in range(4)
            ]
            sig = jax.nn.sigmoid(gate_sum)
            act = gate_sum * sig
            slope = up_sum * sig * (1.0 + gate_sum * (1.0 - sig))
            at = (z * columns + (2 * x + s) * quarter + cc) * 2
            sig_ref[at, :, 0:block] = (hidden * slope).astype(jnp.bfloat16)
            sig_ref[at, :, block : 2 * block] = (sample * slope).astype(jnp.bfloat16)
            sig_ref[at + 1, :, 0:block] = (hidden * act).astype(jnp.bfloat16)
            sig_ref[at + 1, :, block : 2 * block] = (sample * act).astype(jnp.bfloat16)
            return inner

        lax.fori_loop(0, per, one, 0)

    def x_arrivals(d, j):
        for way in (1, -1) if d else (1,):
            origin = z - way * d

            @pl.when(inside(origin))
            def _():
                x_copy(1 - x, origin, j).wait_recv()
                s_copy(1 - x, s, origin, j).start()

    for d in range(n):

        def spread(j, carry, d=d):
            if d == 0:
                produce(j)
                x_copy(x, z, j).start()
                for way in (1, -1):

                    @pl.when(inside(z + way))
                    def _():
                        z_copy(way, 1, j, z).start()

                s_copy(x, s, z, j).start()
                return carry
            for way in (1, -1):
                origin = z - way * d

                @pl.when(inside(origin))
                def _():
                    z_copy(way, d, j, origin).wait_recv()
                    if d < n - 1:

                        @pl.when(inside(z + way))
                        def _():
                            z_copy(way, d + 1, j, origin).start()

                    @pl.when(j >= shared)
                    def _():
                        x_copy(x, origin, j).start()

                    s_copy(x, s, origin, j).start()

            @pl.when(j >= shared)
            def _():
                x_arrivals(d - 1, j)

            return carry

        lax.fori_loop(0, chunks, spread, 0)
        for f in range(shared):
            if d == 0:
                x_copy(1 - x, z, f).wait_recv()
            for way in (1, -1):
                origin = z - way * d

                @pl.when(inside(origin))
                def _():
                    if d > 0:
                        z_copy(way, d, f, origin, True).wait_recv()
                    if d < n - 1:

                        @pl.when(inside(z + way))
                        def _():
                            z_copy(way, d + 1, f, origin, True).start()

                    if d > 0:
                        s_copy(1 - x, s, origin, f).start()
            if d == 0:
                s_copy(1 - x, s, z, f).start()

    def finish(j, carry):
        x_arrivals(n - 1, j)
        return carry

    lax.fori_loop(shared, chunks, finish, 0)

    for d in range(1, n):
        act_copy(d, z).wait_send()
        meta_copy(d, z).wait_send()

    def drain(j, carry):
        sib_part(0, j).wait_send()
        sib_part(1, j).wait_send()
        pair_copy(j).wait_send()
        for d in range(1, n):
            for way in (1, -1):
                origin = z - way * (d - 1)

                @pl.when(inside(origin) & inside(z + way))
                def _():
                    z_copy(way, d, j, origin).wait_send()

                    @pl.when(j < shared)
                    def _():
                        z_copy(way, d, j, origin, True).wait_send()

        for origin in range(n):

            @pl.when((j >= shared) | (z == origin))
            def _():
                x_copy(x, origin, j).wait_send()

            for xq in range(2):
                s_copy(xq, s, origin, j).wait_send()
                s_copy(xq, 1 - s, origin, j).wait_recv()
        return carry

    lax.fori_loop(0, chunks, drain, 0)


def update_kernel(per_step, table_ref, sig_ref, rows_ref, moment_ref, curvature_ref, m_out, c_out, u_out):
    step = pl.program_id(0)
    block = moment_ref.shape[-1]

    def one(u, carry):
        code = table_ref[0, step * per_step + u]
        lhs = rows_ref[code & 15]
        rhs = sig_ref[code >> 4]
        product = jnp.dot(lhs, rhs, preferred_element_type=jnp.float32)
        product = product.astype(jnp.bfloat16).astype(jnp.float32)
        grad, hat = product[:, :block], product[:, block:]
        moment = 0.9 * moment_ref[u].astype(jnp.float32) + (1.0 - 0.9) * grad
        curvature = 0.95 * curvature_ref[u].astype(jnp.float32) + (1.0 - 0.95) * hat * hat
        m_out[u] = moment.astype(jnp.bfloat16)
        c_out[u] = curvature.astype(jnp.bfloat16)
        u_out[u] = jnp.clip(moment / (0.5 * curvature), -1.0, 1.0).astype(jnp.bfloat16)
        return carry

    lax.fori_loop(0, per_step, one, 0, unroll=16 if per_step % 16 == 0 else 1)


def factor_exchange(
    tokens_in, grad_out, sample_grad, gate_tiles, up_tiles, down_tiles,
    block_index, owner_map, slot_map, moment_state, curvature_state,
):
    n = lax.axis_size("dp")
    columns, keep, block, _ = gate_tiles.shape
    local_rows, width = tokens_in.shape
    tokens, blocks = n * local_rows, width // block
    own_cap = moment_state.shape[2]
    quarter = columns // 4
    chunks = 8 if quarter % 8 == 0 else 4
    owner_t, slot_t, index_t = [a.transpose(0, 2, 1) for a in (owner_map, slot_map, block_index)]
    vmem, hbm, smem = (
        pl.BlockSpec(memory_space=pltpu.VMEM),
        pl.BlockSpec(memory_space=pl.ANY),
        pl.BlockSpec(memory_space=pltpu.SMEM),
    )
    bf16, dma = jnp.bfloat16, pltpu.SemaphoreType.DMA
    sig, rows, table = pl.pallas_call(
        functools.partial(signals_kernel, n, chunks, own_cap),
        out_shape=(
            jax.ShapeDtypeStruct((n * columns * 2, tokens, 2 * block), bf16),
            jax.ShapeDtypeStruct((16, block, tokens), bf16),
            jax.ShapeDtypeStruct((1, own_cap), jnp.int32),
        ),
        in_specs=[smem, vmem, vmem, vmem, hbm, hbm, hbm, vmem, vmem, vmem],
        out_specs=(vmem, vmem, vmem),
        scratch_shapes=[
            pltpu.VMEM((3 * blocks, tokens, block), bf16),
            pltpu.VMEM((2, 128, 128), jnp.int32),
            pltpu.VMEM(gate_tiles.shape, bf16),
            pltpu.VMEM(gate_tiles.shape, bf16),
            pltpu.VMEM(gate_tiles.shape, bf16),
            pltpu.VMEM((columns, 4, tokens, block), bf16),
            pltpu.VMEM((2 * quarter, 4, tokens, block), bf16),
            pltpu.VMEM((quarter, 4, tokens, block), bf16),
            pltpu.VMEM((quarter, 4, tokens, block), bf16),
            dma((4, 3)),
            dma((n - 1,)), dma((n - 1,)), dma((n - 1,)), dma((n - 1,)),
            dma((2, chunks)), dma((2, chunks)), dma((chunks,)), dma((chunks,)),
            dma((2, n - 1, chunks + chunks // 4)), dma((2, n - 1, chunks + chunks // 4)),
            dma((n, chunks)), dma((n, chunks)),
            dma((2, n, chunks)), dma((2, n, chunks)),
        ],
        compiler_params=pltpu.CompilerParams(
            collective_id=0, has_side_effects=True, vmem_limit_bytes=VMEM_BYTES
        ),
        name="signals",
    )(
        index_t, tokens_in, grad_out, sample_grad,
        gate_tiles, up_tiles, down_tiles, owner_t, slot_t, index_t,
    )
    per_step = max(p for p in range(1, 65) if own_cap % p == 0)
    state = pl.BlockSpec((per_step, block, block), lambda i, t: (i, 0, 0))
    once = pl.Buffered(1)
    outs = pl.pallas_call(
        functools.partial(update_kernel, per_step),
        out_shape=[jax.ShapeDtypeStruct((own_cap, block, block), bf16)] * 3,
        grid_spec=pltpu.PrefetchScalarGridSpec(
            num_scalar_prefetch=1,
            grid=(own_cap // per_step,),
            in_specs=[
                pl.BlockSpec(sig.shape, lambda i, t: (0, 0, 0), pipeline_mode=once),
                pl.BlockSpec(rows.shape, lambda i, t: (0, 0, 0), pipeline_mode=once),
                state,
                state,
            ],
            out_specs=[state] * 3,
        ),
        compiler_params=pltpu.CompilerParams(vmem_limit_bytes=VMEM_BYTES),
        name="update",
    )(
        table, sig, rows,
        moment_state.reshape(own_cap, block, block),
        curvature_state.reshape(own_cap, block, block),
    )
    return tuple(out.reshape(moment_state.shape) for out in outs)


momentum_decay = 0.9
curvature_decay = 0.95
curvature_scale = 0.5


def pick_blocks(matrix, row_list, block_size):
    shaped = matrix.reshape(matrix.shape[0], matrix.shape[1] // block_size, block_size)
    chosen = row_list[..., None] == jnp.arange(shaped.shape[1], dtype=row_list.dtype)
    return jnp.einsum("tbd,ckb->tckd", shaped, chosen.astype(matrix.dtype))


def backward_signals(summed):
    hidden_width = summed.shape[1] // 4
    gate_sum = summed[:, 0:hidden_width]
    up_sum = summed[:, hidden_width : 2 * hidden_width]
    hidden_grad = summed[:, 2 * hidden_width : 3 * hidden_width]
    sample_hidden = summed[:, 3 * hidden_width : 4 * hidden_width]
    sigmoid_gate = jax.nn.sigmoid(gate_sum)
    activation = gate_sum * sigmoid_gate
    gate_slope = up_sum * sigmoid_gate * (1.0 + gate_sum * (1.0 - sigmoid_gate))
    return jnp.concatenate(
        [
            hidden_grad * gate_slope,
            hidden_grad * activation,
            sample_hidden * gate_slope,
            sample_hidden * activation,
        ],
        axis=1,
    ).astype(jnp.bfloat16)


def tile_exchange(
    tokens_in,
    grad_out,
    sample_grad,
    gate_tiles,
    up_tiles,
    down_tiles,
    block_index,
    owner_map,
    slot_map,
    moment_state,
    curvature_state,
):
    block_size = gate_tiles.shape[-1]
    column_count = gate_tiles.shape[0]
    band_blocks = tokens_in.shape[1] // block_size
    hidden_width = column_count * block_size
    all_tokens, all_grads, all_samples = (
        lax.all_gather(tokens_in, "dp", axis=0, tiled=True),
        lax.all_gather(grad_out, "dp", axis=0, tiled=True),
        lax.all_gather(sample_grad, "dp", axis=0, tiled=True),
    )
    token_count = all_tokens.shape[0]
    local_rows = block_index - lax.axis_index(("mp", "sub")) * band_blocks
    token_rows = all_tokens
    gate_part = jnp.einsum(
        "tckd,ckde->tce",
        pick_blocks(token_rows, local_rows[0], block_size),
        gate_tiles,
        preferred_element_type=jnp.float32,
    )
    up_part = jnp.einsum(
        "tckd,ckde->tce",
        pick_blocks(token_rows, local_rows[1], block_size),
        up_tiles,
        preferred_element_type=jnp.float32,
    )
    down_part = jnp.einsum(
        "tckd,cked->tce",
        pick_blocks(all_grads, local_rows[2], block_size),
        down_tiles,
        preferred_element_type=jnp.float32,
    )
    sample_part = jnp.einsum(
        "tckd,cked->tce",
        pick_blocks(all_samples, local_rows[2], block_size),
        down_tiles,
        preferred_element_type=jnp.float32,
    )
    summed = lax.psum(
        jnp.concatenate([gate_part, up_part, down_part, sample_part], axis=1)
        .reshape(token_count, 4 * hidden_width)
        .astype(jnp.bfloat16),
        ("mp", "sub"),
    ).astype(jnp.float32)
    shard_rows = backward_signals(summed)
    row_count = shard_rows.shape[0]
    token_rows = all_tokens
    gate_rows = pick_blocks(token_rows, local_rows[0], block_size)
    up_rows = pick_blocks(token_rows, local_rows[1], block_size)
    signals = shard_rows.reshape(row_count, 4, column_count, block_size)
    grad_gate = jnp.einsum(
        "tckd,tce->ckde", gate_rows, signals[:, 0], preferred_element_type=jnp.float32
    )
    grad_up = jnp.einsum(
        "tckd,tce->ckde", up_rows, signals[:, 1], preferred_element_type=jnp.float32
    )
    hat_gate = jnp.einsum(
        "tckd,tce->ckde", gate_rows, signals[:, 2], preferred_element_type=jnp.float32
    )
    hat_up = jnp.einsum(
        "tckd,tce->ckde", up_rows, signals[:, 3], preferred_element_type=jnp.float32
    )
    totals = jnp.stack([jnp.stack([grad_gate, grad_up]), jnp.stack([hat_gate, hat_up])])
    tile_list = jnp.transpose(totals.astype(jnp.bfloat16), (1, 2, 3, 0, 4, 5)).reshape(
        -1, 2, block_size, block_size
    )
    tile_total = tile_list.shape[0]
    owner_count = lax.axis_size("dp")
    own_cap = moment_state.shape[2]
    send_cap = max(2, 2 * (tile_total // owner_count))
    owners = owner_map.reshape(-1)
    slot_list = slot_map.reshape(-1)
    same_owner = owners[:, None] == owners[None, :]
    earlier = jnp.arange(tile_total)[None, :] < jnp.arange(tile_total)[:, None]
    send_rank = jnp.sum((same_owner & earlier).astype(jnp.int32), axis=1)
    position = owners * send_cap + send_rank
    payload = (
        jnp.zeros((owner_count * send_cap, 2, block_size, block_size), jnp.bfloat16)
        .at[position]
        .set(tile_list)
    )
    slot_ids = jnp.full((owner_count * send_cap,), own_cap, jnp.int32).at[position].set(slot_list)
    received, received_ids = (
        lax.all_to_all(
            payload.reshape(owner_count, send_cap, 2, block_size, block_size),
            "dp",
            split_axis=0,
            concat_axis=0,
            tiled=True,
        ),
        lax.all_to_all(
            slot_ids.reshape(owner_count, send_cap), "dp", split_axis=0, concat_axis=0, tiled=True
        ),
    )
    placed = jnp.zeros((own_cap + 1, 2, block_size, block_size), jnp.bfloat16)
    placed = placed.at[received_ids.reshape(-1)].set(
        received.reshape(-1, 2, block_size, block_size)
    )[:own_cap]
    grad_state = placed[:, 0].astype(jnp.float32)
    hat_state = placed[:, 1].astype(jnp.float32)
    state_shape = moment_state.shape
    moment = (
        momentum_decay * moment_state.reshape(own_cap, block_size, block_size).astype(jnp.float32)
        + (1.0 - momentum_decay) * grad_state
    )
    curvature = (
        curvature_decay
        * curvature_state.reshape(own_cap, block_size, block_size).astype(jnp.float32)
        + (1.0 - curvature_decay) * hat_state * hat_state
    )
    update = jnp.clip(moment / (curvature_scale * curvature), -1.0, 1.0)
    return (
        moment.astype(jnp.bfloat16).reshape(state_shape),
        curvature.astype(jnp.bfloat16).reshape(state_shape),
        update.astype(jnp.bfloat16).reshape(state_shape),
    )


def solution(mesh):
    in_specs = (
        P(("groups", "dp"), ("mp", "sub")),
        P(("groups", "dp"), ("mp", "sub")),
        P(("groups", "dp"), ("mp", "sub")),
        P(("groups", "dp"), ("mp", "sub"), None, None),
        P(("groups", "dp"), ("mp", "sub"), None, None),
        P(("groups", "dp"), ("mp", "sub"), None, None),
        P("groups", "dp", ("mp", "sub")),
        P("groups", "dp", ("mp", "sub")),
        P("groups", "dp", ("mp", "sub")),
        P(("groups", "dp"), ("mp", "sub"), None, None, None),
        P(("groups", "dp"), ("mp", "sub"), None, None, None),
    )
    out_specs = (
        P(("groups", "dp"), ("mp", "sub"), None, None, None),
        P(("groups", "dp"), ("mp", "sub"), None, None, None),
        P(("groups", "dp"), ("mp", "sub"), None, None, None),
    )
    factors = mesh.shape["mp"] == 2 and mesh.shape["sub"] == 2

    def on_device(*args):
        columns, _, block_size, _ = args[3].shape
        tokens = args[0].shape[0] * mesh.shape["dp"]
        own_cap = args[9].shape[2]
        fits = tokens <= block_size and columns % 16 == 0 and own_cap % 16 == 0
        fits = fits and columns <= 128 and 2 * args[3].shape[1] * mesh.shape["dp"] <= 128
        return (factor_exchange if factors and fits else tile_exchange)(*args)

    return jax.shard_map(
        on_device, mesh=mesh, in_specs=in_specs, out_specs=out_specs, check_vma=False
    )
```
